128 devices in a mesh: wide: 16 (over x_hi, z, core), narrow: 8 (over x_lo, y).
Axes of the slice: x: 4 (x_hi: 2, x_lo: 2; x = x_hi * 2 + x_lo), y: 4, z: 4, core: 2. Of those that a mesh axis runs over, the one named last changes fastest.
Arguments:
- alignment: bfloat16 [128, 1536, 256], P(('wide', 'narrow')), may hold values from -6 to 6
- w_query: bfloat16 [256, 256], replicated, may hold values from -0.375 to 0.375
- w_key: bfloat16 [256, 256], replicated, may hold values from -0.375 to 0.375
- w_value: bfloat16 [256, 256], replicated, may hold values from -0.375 to 0.375
- w_gate: bfloat16 [256, 256], replicated, may hold values from -0.375 to 0.375
- w_attend: bfloat16 [256, 256], replicated, may hold values from -0.75 to 0.75
- w_left: bfloat16 [256, 32], replicated, may hold values from -0.375 to 0.375
- w_right: bfloat16 [256, 32], replicated, may hold values from -0.375 to 0.375
- w_pair: bfloat16 [1024, 128], replicated, may hold values from -1.5 to 1.5
Outputs:
- alignment_out: bfloat16 [128, 1536, 256], P(('wide', 'narrow'))
- pair_update: bfloat16 [1536, 1536, 128], P('wide', 'narrow')
The draws below stay inside these ranges and needn't reach their ends.
All inputs are finite; a program needn't handle non-finite values.
Results may differ from the reference program's by a relative error of at most 0.02.
Values may be sent and summed in bfloat16 or wider, within the bound.
No kernel may reach another device: no remote copies, remote signals or barrier semaphores. Data moves between devices by JAX's collectives and lax.ppermute only.
A program may use at most 128 MiB of HBM per device.

```python
import jax
import jax.numpy as jnp
from jax import lax

C_M = 256
HEADS = 8
HEAD_DIM = 32
C_OPM = 32
C_Z = 128
SEQS = 128
RESIDUES = 1536


def block_levels(own_key, shape, cuts, smallest, largest):
    factor_of = 1.0
    for position, blocks in cuts:
        heights = jax.random.uniform(jax.random.fold_in(jax.random.fold_in(own_key, 6), position), (blocks,), jnp.float32, smallest / len(cuts), largest / len(cuts))
        factor_of = factor_of * jnp.repeat(jnp.exp(heights), shape[position] // blocks).reshape((-1,) + (1,) * (len(shape) - 1 - position))
    return factor_of


def noise(own_key, dims, scale, bound, pieces=(), held_as=jnp.bfloat16):
    factor_of = block_levels(own_key, dims, pieces, -0.22, 0.18) if pieces else 1.0
    result = jax.random.normal(own_key, dims, jnp.float32) * scale * factor_of
    return jnp.minimum(jnp.maximum(result, -bound), bound).astype(held_as)


def setup_inputs(seed: int = 0) -> dict:
    seeds = jax.random.split(jax.random.key(seed), 10)
    return {
        "alignment": noise(seeds[0], (SEQS, RESIDUES, C_M), 1.0, 6.0, ((0, 128),)),
        "w_query": noise(seeds[1], (C_M, C_M), C_M ** -0.5, 0.375),
        "w_key": noise(seeds[2], (C_M, C_M), C_M ** -0.5, 0.375),
        "w_value": noise(seeds[3], (C_M, C_M), C_M ** -0.5, 0.375),
        "w_gate": noise(seeds[4], (C_M, C_M), C_M ** -0.5, 0.375),
        "w_attend": noise(seeds[5], (C_M, C_M), (C_M // 4) ** -0.5, 0.75),
        "w_left": noise(seeds[6], (C_M, C_OPM), C_M ** -0.5, 0.375),
        "w_right": noise(seeds[7], (C_M, C_OPM), C_M ** -0.5, 0.375),
        "w_pair": noise(seeds[8], (C_OPM * C_OPM, C_Z), (C_OPM * C_OPM // 64) ** -0.5, 1.5),
    }


def layer_norm(values):
    values = values.astype(jnp.float32)
    average = lax.optimization_barrier(jnp.mean(values, axis=-1, keepdims=True))
    centered = values - average
    variance = lax.optimization_barrier(jnp.mean(centered * centered, axis=-1, keepdims=True))
    return (centered * lax.rsqrt(variance + 1e-05)).astype(jnp.bfloat16)

def attend_block(block, w_query, w_key, w_value, w_gate, w_attend):
    normed = layer_norm(block)
    seq_all, res_blk, width = block.shape
    query_rows = jnp.dot(normed, w_query, preferred_element_type=jnp.float32).astype(jnp.bfloat16)
    key_rows = jnp.dot(normed, w_key, preferred_element_type=jnp.float32).astype(jnp.bfloat16)
    value_rows = jnp.dot(normed, w_value, preferred_element_type=jnp.float32).astype(jnp.bfloat16)
    gate_act = jax.nn.sigmoid(jnp.dot(normed, w_gate, preferred_element_type=jnp.float32))
    query_f = query_rows.astype(jnp.float32).reshape(seq_all, res_blk, HEADS, HEAD_DIM)
    key_f = key_rows.astype(jnp.float32).reshape(seq_all, res_blk, HEADS, HEAD_DIM)
    value_f = value_rows.astype(jnp.float32).reshape(seq_all, res_blk, HEADS, HEAD_DIM)
    scores = jnp.einsum('srhd,trhd->rhst', query_f, key_f) * HEAD_DIM ** (-0.5)
    weighted = lax.optimization_barrier(jnp.exp(scores).astype(jnp.bfloat16))
    weighted_f = weighted.astype(jnp.float32)
    denominator = lax.optimization_barrier(jnp.sum(weighted_f, axis=-1))
    numerator = jnp.einsum('rhst,trhd->srhd', weighted_f, value_f)
    gate_heads = gate_act.reshape(seq_all, res_blk, HEADS, HEAD_DIM)
    attended = gate_heads * numerator / jnp.transpose(denominator, (2, 0, 1))[..., None]
    attended = attended.reshape(seq_all, res_blk, width).astype(jnp.bfloat16)
    update = jnp.dot(attended, w_attend, preferred_element_type=jnp.float32)
    return (block.astype(jnp.float32) + update).astype(jnp.bfloat16)

def reference(alignment, w_query, w_key, w_value, w_gate, w_attend, w_left, w_right, w_pair):
    blocks = alignment.reshape(SEQS, RESIDUES // 8, 8, C_M).transpose(1, 0, 2, 3)
    updated = lax.map(lambda block: attend_block(block, w_query, w_key, w_value, w_gate, w_attend), blocks)
    alignment_out = updated.transpose(1, 0, 2, 3).reshape(SEQS, RESIDUES, C_M)
    normed_two = layer_norm(alignment_out)
    left_rows = jnp.dot(normed_two, w_left, preferred_element_type=jnp.float32).astype(jnp.bfloat16)
    right_rows = jnp.dot(normed_two, w_right, preferred_element_type=jnp.float32).astype(jnp.bfloat16)
    right_f = right_rows.astype(jnp.float32)
    left_blocks = left_rows.reshape(SEQS, RESIDUES // 8, 8, C_OPM).transpose(1, 0, 2, 3)

    def pair_block(left_block):
        outer_prod = jnp.einsum('sic,sje->ijce', left_block.astype(jnp.float32), right_f) / SEQS
        outer_prod = outer_prod.astype(jnp.bfloat16).reshape(8, RESIDUES, C_OPM * C_OPM)
        return jnp.dot(outer_prod, w_pair, preferred_element_type=jnp.float32).astype(jnp.bfloat16)
    pair_update = lax.map(pair_block, left_blocks).reshape(RESIDUES, RESIDUES, C_Z)
    return (alignment_out, pair_update)
```

```python
import functools

import jax
import jax.numpy as jnp
from jax import lax
from jax.experimental import pallas as pl
from jax.experimental.pallas import tpu as pltpu
from jax.sharding import Mesh, PartitionSpec as P

HEADS = 8
HEAD_DIM = 32
OPM = 32
SEQS = 128
WIDTH = 256
LANES = 128
AXES = ("x_hi", "z", "core", "x_lo", "y")
SIZES = (2, 4, 2, 2, 4)
BLK = 12
ROWS = 2 * BLK
PEERS = 8
VMEM = pltpu.CompilerParams(vmem_limit_bytes=50 * 1024 * 1024)
F32 = jnp.float32
BF16 = jnp.bfloat16
NT = (((1,), (1,)), ((), ()))


def block_of(device):
    y, rest = device % 4, device // 4
    x_lo, rest = rest % 2, rest // 2
    core, rest = rest % 2, rest // 2
    z, x_hi = rest % 4, rest // 4
    return (x_lo * 4 + y) * 16 + core * 8 + x_hi * 4 + z


BLOCK_OF = [block_of(d) for d in range(SEQS)]
DEVICE_OF = [BLOCK_OF.index(b) for b in range(SEQS)]


def vmem_spec():
    return pl.BlockSpec(memory_space=pltpu.VMEM)


def normalise(values):
    average = jnp.mean(values, axis=-1, keepdims=True)
    centered = values - average
    variance = jnp.mean(centered * centered, axis=-1, keepdims=True)
    return (centered * lax.rsqrt(variance + 1e-05)).astype(BF16)


def pack_kernel(x_ref, out_ref):
    for group in range(SEQS // 4):
        rows = x_ref[group * 48 : group * 48 + 48, :].astype(F32)
        for part in range(4):
            piece = rows[part * BLK : part * BLK + BLK]
            both = jnp.concatenate([piece[:, :LANES], piece[:, LANES:]], axis=0)
            out_ref[DEVICE_OF[group * 4 + part]] = both.astype(BF16)


def unpack_kernel(x_ref, out_ref):
    for group in range(SEQS // 4):
        pieces = [x_ref[DEVICE_OF[group * 4 + part]].astype(F32) for part in range(4)]
        left = jnp.concatenate([piece[:BLK] for piece in pieces], axis=0)
        right = jnp.concatenate([piece[BLK:] for piece in pieces], axis=0)
        out_ref[group * 48 : group * 48 + 48, :] = jnp.concatenate([left, right], axis=1).astype(BF16)


def attention_kernel(
    x_ref, wq_ref, wk_ref, wv_ref, wg_ref, wa_ref, wlr_ref, u_ref, lt_ref, rt_ref,
    flat, normed, query, key, value, gate, attended, update,
):
    flat[...] = x_ref[...].astype(F32).reshape(SEQS * ROWS, LANES)

    def residue(r):
        return jnp.concatenate(
            [flat[pl.ds(r, SEQS, stride=ROWS), :], flat[pl.ds(BLK + r, SEQS, stride=ROWS), :]], axis=1
        )

    def span(r):
        return pl.ds(pl.multiple_of(r * SEQS, SEQS), SEQS)

    for r in range(BLK):
        normed[span(r), :] = normalise(residue(r))
    rows = normed[...]
    query[...] = jnp.dot(rows, wq_ref[...], preferred_element_type=F32).astype(BF16)
    key[...] = jnp.dot(rows, wk_ref[...], preferred_element_type=F32).astype(BF16)
    value[...] = jnp.dot(rows, wv_ref[...], preferred_element_type=F32).astype(BF16)
    gate[...] = jax.nn.sigmoid(jnp.dot(rows, wg_ref[...], preferred_element_type=F32))

    lane = lax.broadcasted_iota(jnp.int32, (SEQS, WIDTH), 1) // HEAD_DIM
    own = [(lane == h) for h in range(HEADS)]
    zero = jnp.zeros((SEQS, WIDTH), BF16)
    ones = jnp.concatenate([jnp.where(m, 1.0, 0.0).astype(BF16) for m in own], axis=0)

    def attend(r, carry):
        at = span(r)
        q, k, v = query[at, :], key[at, :], value[at, :]
        k_heads = jnp.concatenate([jnp.where(m, k, zero) for m in own], axis=0)
        v_heads = jnp.concatenate([jnp.where(m, v, zero) for m in own], axis=0)
        scores = lax.dot_general(q, k_heads, NT, preferred_element_type=F32) * HEAD_DIM ** (-0.5)
        weighted = jnp.exp(scores).astype(BF16)
        numerator = jnp.dot(weighted, v_heads, preferred_element_type=F32)
        denominator = jnp.dot(weighted, ones, preferred_element_type=F32)
        attended[at, :] = (gate[at, :] * numerator / denominator).astype(BF16)
        return carry

    lax.fori_loop(0, BLK, attend, 0)
    update[...] = jnp.dot(attended[...], wa_ref[...], preferred_element_type=F32)
    for r in range(BLK):
        updated = (residue(r) + update[span(r), :]).astype(BF16).astype(F32)
        flat[pl.ds(r, SEQS, stride=ROWS), :] = updated[:, :LANES]
        flat[pl.ds(BLK + r, SEQS, stride=ROWS), :] = updated[:, LANES:]
        normed[span(r), :] = normalise(updated)
    sides = lax.dot_general(wlr_ref[...], normed[...], NT, preferred_element_type=F32).astype(BF16)
    for r in range(BLK):
        lt_ref[r * OPM : (r + 1) * OPM, :] = sides[:OPM, r * SEQS : (r + 1) * SEQS]
        rt_ref[r * OPM : (r + 1) * OPM, :] = sides[OPM:, r * SEQS : (r + 1) * SEQS]
    u_ref[...] = flat[...].reshape(SEQS, ROWS, LANES).astype(BF16)


def attention(x, wq, wk, wv, wg, wa, wlr):
    tall = SEQS * BLK
    return pl.pallas_call(
        attention_kernel,
        out_shape=(
            jax.ShapeDtypeStruct((SEQS, ROWS, LANES), BF16),
            jax.ShapeDtypeStruct((BLK * OPM, SEQS), BF16),
            jax.ShapeDtypeStruct((BLK * OPM, SEQS), BF16),
        ),
        in_specs=[vmem_spec()] * 7,
        out_specs=(vmem_spec(),) * 3,
        scratch_shapes=[
            pltpu.VMEM((SEQS * ROWS, LANES), F32),
            pltpu.VMEM((tall, WIDTH), BF16),
            pltpu.VMEM((tall, WIDTH), BF16),
            pltpu.VMEM((tall, WIDTH), BF16),
            pltpu.VMEM((tall, WIDTH), BF16),
            pltpu.VMEM((tall, WIDTH), F32),
            pltpu.VMEM((tall, WIDTH), BF16),
            pltpu.VMEM((tall, WIDTH), F32),
        ],
        compiler_params=VMEM,
        name="attention",
    )(x, wq, wk, wv, wg, wa, wlr)


def pair_kernel(at_ref, l_ref, own_ref, other_ref, we_ref, wo_ref, out_ref, flat, right, outer):
    cols = 192
    half = PEERS * BLK * OPM

    @pl.when(pl.program_id(0) == 0)
    def _():
        first = pl.multiple_of(at_ref[1] * half, half)
        flat[pl.ds(first, half), :] = own_ref[...].astype(F32)
        flat[pl.ds(pl.multiple_of(half - first, half), half), :] = other_ref[...].astype(F32)
        for p in range(OPM // 2):
            even = flat[pl.ds(2 * p, cols, stride=OPM), :]
            odd = flat[pl.ds(2 * p + 1, cols, stride=OPM), :]
            right[p] = jnp.concatenate([even, odd], axis=0).T.astype(BF16)

    left = l_ref[0]
    for p in range(OPM // 2):
        product = jnp.dot(left, right[p], preferred_element_type=F32).astype(BF16)
        for i in range(BLK):
            outer[i, p * OPM : (p + 1) * OPM, :] = product[i * OPM : (i + 1) * OPM]
    even_w, odd_w = we_ref[...], wo_ref[...]
    for i in range(BLK):
        even = jnp.dot(even_w, outer[i, :, :256], preferred_element_type=F32)
        odd = jnp.dot(odd_w, outer[i, :, 128:], preferred_element_type=F32)
        total = (even[:, :cols] + odd[:, 64:]) * (1.0 / SEQS)
        out_ref[i] = total.T.astype(BF16)


def pair_grid(place, left, own, other, w_even, w_odd):
    half = PEERS * BLK * OPM
    return pl.pallas_call(
        pair_kernel,
        out_shape=jax.ShapeDtypeStruct((PEERS * BLK, 192, 128), BF16),
        grid_spec=pltpu.PrefetchScalarGridSpec(
            num_scalar_prefetch=1,
            grid=(PEERS,),
            in_specs=[
                pl.BlockSpec((1, BLK * OPM, SEQS), lambda k, at: (k, 0, 0)),
                pl.BlockSpec((half, SEQS), lambda k, at: (0, 0)),
                pl.BlockSpec((half, SEQS), lambda k, at: (0, 0)),
                pl.BlockSpec((128, 512), lambda k, at: (0, 0)),
                pl.BlockSpec((128, 512), lambda k, at: (0, 0)),
            ],
            out_specs=pl.BlockSpec((BLK, 192, 128), lambda k, at: (k ^ at[0], 0, 0)),
            scratch_shapes=[
                pltpu.VMEM((2 * half, SEQS), F32),
                pltpu.VMEM((OPM // 2, SEQS, 384), BF16),
                pltpu.VMEM((BLK, 512, 384), BF16),
            ],
        ),
        compiler_params=VMEM,
        name="pair_grid",
    )(place, left, own, other, w_even, w_odd)


def left_route(step):
    pairs = []
    for d in range(SEQS):
        y, x_lo, core, z, x_hi = d % 4, d // 4 % 2, d // 8 % 2, d // 16 % 4, d // 64
        place = (x_hi * 4 + z) ^ step
        pairs.append((d, ((x_lo * 4 + y) * 2 + core) * 8 + place))
    return pairs


def body(alignment, w_query, w_key, w_value, w_gate, w_attend, w_left, w_right, w_pair):
    one = jax.ShapeDtypeStruct((SEQS, ROWS, LANES), BF16)
    packed = pl.pallas_call(
        pack_kernel, out_shape=one, in_specs=[vmem_spec()], out_specs=vmem_spec(),
        compiler_params=VMEM, name="pack",
    )(alignment[0])
    blocks = lax.all_to_all(packed, AXES, split_axis=0, concat_axis=0, tiled=True)
    w_sides = jnp.concatenate([w_left, w_right], axis=1).T
    updated, left, right = attention(blocks, w_query, w_key, w_value, w_gate, w_attend, w_sides)

    copies = jnp.broadcast_to(right[None], (PEERS,) + right.shape)
    own = lax.all_to_all(copies, ("x_hi", "z"), split_axis=0, concat_axis=0, tiled=True)
    own = own.reshape(PEERS * BLK * OPM, SEQS)
    other = lax.ppermute(own, "core", [(0, 1), (1, 0)])
    lefts = jnp.stack([lax.ppermute(left, AXES, left_route(k)) for k in range(PEERS)])

    returned = lax.all_to_all(updated, AXES, split_axis=0, concat_axis=0, tiled=True)
    weights = w_pair.reshape(OPM, OPM // 2, 2, 128).transpose(2, 3, 1, 0).reshape(2, 128, 512)
    place = jnp.stack([lax.axis_index(("x_lo", "y")), lax.axis_index("core")]).astype(jnp.int32)
    pair_update = pair_grid(place, lefts, own, other, weights[0], weights[1])
    alignment_out = pl.pallas_call(
        unpack_kernel, out_shape=jax.ShapeDtypeStruct(alignment.shape[1:], BF16),
        in_specs=[vmem_spec()], out_specs=vmem_spec(), compiler_params=VMEM, name="unpack",
    )(returned)
    return (alignment_out[None], pair_update)


def solution(mesh):
    fine = Mesh(mesh.devices.reshape(SIZES), AXES)
    placed = (P(AXES, None, None),) + (P(),) * 8
    return jax.shard_map(
        body,
        mesh=fine,
        in_specs=placed,
        out_specs=(P(AXES, None, None), P(AXES[:3], AXES[3:], None)),
        check_vma=False,
    )
```

```python
import functools

import jax
import jax.numpy as jnp
from jax import lax
from jax.experimental import pallas as pl
from jax.experimental.pallas import tpu as pltpu
from jax.sharding import Mesh, PartitionSpec as P

HEADS = 8
HEAD_DIM = 32
OPM = 32
SEQS = 128
WIDTH = 256
LANES = 128
AXES = ("x_hi", "z", "core", "x_lo", "y")
SIZES = (2, 4, 2, 2, 4)
BLK = 12
ROWS = 2 * BLK
PEERS = 8
VMEM = pltpu.CompilerParams(vmem_limit_bytes=24 * 1024 * 1024)
F32 = jnp.float32
BF16 = jnp.bfloat16
NT = (((1,), (1,)), ((), ()))


def block_of(device):
    y, rest = device % 4, device // 4
    x_lo, rest = rest % 2, rest // 2
    core, rest = rest % 2, rest // 2
    z, x_hi = rest % 4, rest // 4
    return (x_lo * 4 + y) * 16 + core * 8 + x_hi * 4 + z


BLOCK_OF = [block_of(d) for d in range(SEQS)]
DEVICE_OF = [BLOCK_OF.index(b) for b in range(SEQS)]


def vmem_spec():
    return pl.BlockSpec(memory_space=pltpu.VMEM)


def normalise(values):
    average = jnp.mean(values, axis=-1, keepdims=True)
    centered = values - average
    variance = jnp.mean(centered * centered, axis=-1, keepdims=True)
    return (centered * lax.rsqrt(variance + 1e-05)).astype(BF16)


def pack_kernel(x_ref, out_ref):
    for group in range(SEQS // 4):
        rows = x_ref[group * 48 : group * 48 + 48, :].astype(F32)
        for part in range(4):
            piece = rows[part * BLK : part * BLK + BLK]
            both = jnp.concatenate([piece[:, :LANES], piece[:, LANES:]], axis=0)
            out_ref[DEVICE_OF[group * 4 + part]] = both.astype(BF16)


def unpack_kernel(x_ref, out_ref):
    for group in range(SEQS // 4):
        pieces = [x_ref[DEVICE_OF[group * 4 + part]].astype(F32) for part in range(4)]
        left = jnp.concatenate([piece[:BLK] for piece in pieces], axis=0)
        right = jnp.concatenate([piece[BLK:] for piece in pieces], axis=0)
        out_ref[group * 48 : group * 48 + 48, :] = jnp.concatenate([left, right], axis=1).astype(BF16)


def attention_kernel(
    x_ref, w_ref, wlr_ref, u_ref, lt_ref, rt_ref,
    flat, normed, query, key, value, gate, attended, update,
):
    flat[...] = x_ref[...].astype(F32).reshape(SEQS * ROWS, LANES)

    def residue(r):
        return jnp.concatenate(
            [flat[pl.ds(r, SEQS, stride=ROWS), :], flat[pl.ds(BLK + r, SEQS, stride=ROWS), :]], axis=1
        )

    def span(r):
        return pl.ds(r * SEQS, SEQS)

    for r in range(BLK):
        normed[span(r), :] = normalise(residue(r))
    rows = normed[...]
    query[...] = jnp.dot(rows, w_ref[0], preferred_element_type=F32).astype(BF16)
    key[...] = jnp.dot(rows, w_ref[1], preferred_element_type=F32).astype(BF16)
    value[...] = jnp.dot(rows, w_ref[2], preferred_element_type=F32).astype(BF16)
    gate[...] = jax.nn.sigmoid(jnp.dot(rows, w_ref[3], preferred_element_type=F32))

    lane = lax.broadcasted_iota(jnp.int32, (SEQS, WIDTH), 1) // HEAD_DIM
    own = [(lane == h) for h in range(HEADS)]
    zero = jnp.zeros((SEQS, WIDTH), BF16)
    ones = jnp.concatenate([jnp.where(m, 1.0, 0.0).astype(BF16) for m in own], axis=0)

    for r in range(BLK):
        at = span(r)
        q, k, v = query[at, :], key[at, :], value[at, :]
        k_heads = jnp.concatenate([jnp.where(m, k, zero) for m in own], axis=0)
        v_heads = jnp.concatenate([jnp.where(m, v, zero) for m in own], axis=0)
        scores = lax.dot_general(q, k_heads, NT, preferred_element_type=F32) * HEAD_DIM ** (-0.5)
        weighted = jnp.exp(scores).astype(BF16)
        numerator = jnp.dot(weighted, v_heads, preferred_element_type=F32)
        denominator = jnp.dot(weighted, ones, preferred_element_type=F32)
        attended[at, :] = (gate[at, :] * numerator / denominator).astype(BF16)

    update[...] = jnp.dot(attended[...], w_ref[4], preferred_element_type=F32)
    for r in range(BLK):
        updated = (residue(r) + update[span(r), :]).astype(BF16).astype(F32)
        flat[pl.ds(r, SEQS, stride=ROWS), :] = updated[:, :LANES]
        flat[pl.ds(BLK + r, SEQS, stride=ROWS), :] = updated[:, LANES:]
        normed[span(r), :] = normalise(updated)
    sides = lax.dot_general(wlr_ref[...], normed[...], NT, preferred_element_type=F32).astype(BF16)
    for r in range(BLK):
        lt_ref[r * OPM : (r + 1) * OPM, :] = sides[:OPM, r * SEQS : (r + 1) * SEQS]
        for copy in range(PEERS):
            rt_ref[copy, r * OPM : (r + 1) * OPM, :] = sides[OPM:, r * SEQS : (r + 1) * SEQS]
    u_ref[...] = flat[...].reshape(SEQS, ROWS, LANES).astype(BF16)


def attention(x, weights, wlr):
    tall = SEQS * BLK
    return pl.pallas_call(
        attention_kernel,
        out_shape=(
            jax.ShapeDtypeStruct((SEQS, ROWS, LANES), BF16),
            jax.ShapeDtypeStruct((BLK * OPM, SEQS), BF16),
            jax.ShapeDtypeStruct((PEERS, BLK * OPM, SEQS), BF16),
        ),
        in_specs=[vmem_spec()] * 3,
        out_specs=(vmem_spec(),) * 3,
        scratch_shapes=[
            pltpu.VMEM((SEQS * ROWS, LANES), F32),
            pltpu.VMEM((tall, WIDTH), BF16),
            pltpu.VMEM((tall, WIDTH), BF16),
            pltpu.VMEM((tall, WIDTH), BF16),
            pltpu.VMEM((tall, WIDTH), BF16),
            pltpu.VMEM((tall, WIDTH), F32),
            pltpu.VMEM((tall, WIDTH), BF16),
            pltpu.VMEM((tall, WIDTH), F32),
        ],
        compiler_params=VMEM,
        name="attention",
    )(x, weights, wlr)


COLS = 192
HALF = PEERS * BLK * OPM


def pair_rows(left, right, we_ref, wo_ref, out_ref, outer):
    for p in range(OPM // 2):
        product = jnp.dot(left, right[p], preferred_element_type=F32).astype(BF16)
        for i in range(BLK):
            outer[i, p * OPM : (p + 1) * OPM, :] = product[i * OPM : (i + 1) * OPM]
    even_w, odd_w = we_ref[...], wo_ref[...]
    for i in range(BLK):
        even = jnp.dot(even_w, outer[i, :, :256], preferred_element_type=F32)
        odd = jnp.dot(odd_w, outer[i, :, 128:], preferred_element_type=F32)
        total = (even.T[:COLS] + odd.T[64:]) * (1.0 / SEQS)
        out_ref[i] = total.astype(BF16)


def first_pair_kernel(at_ref, l_ref, own_ref, other_ref, we_ref, wo_ref, out_ref, right, flat, outer):
    first = pl.multiple_of(at_ref[2] * HALF, HALF)
    flat[pl.ds(first, HALF), :] = own_ref[...].astype(F32)
    flat[pl.ds(pl.multiple_of(HALF - first, HALF), HALF), :] = other_ref[...].astype(F32)
    for p in range(OPM // 2):
        even = flat[pl.ds(2 * p, COLS, stride=OPM), :]
        odd = flat[pl.ds(2 * p + 1, COLS, stride=OPM), :]
        right[p] = jnp.concatenate([even, odd], axis=0).T.astype(BF16)
    pair_rows(l_ref[0], right, we_ref, wo_ref, out_ref, outer)


def next_pair_kernel(at_ref, l_ref, right, we_ref, wo_ref, before_ref, out_ref, outer):
    pair_rows(l_ref[0], right, we_ref, wo_ref, out_ref, outer)


def whole(*shape):
    return pl.BlockSpec(shape, lambda k, at: (0,) * len(shape))


def pair_call(kernel, where, steps, operands, in_specs, extra_shapes, extra_specs, scratch, aliases):
    flops = 2 * steps * BLK * COLS * OPM * OPM * (SEQS + 128)
    return pl.pallas_call(
        kernel,
        out_shape=[jax.ShapeDtypeStruct((PEERS * BLK, COLS, 128), BF16)] + extra_shapes,
        grid_spec=pltpu.PrefetchScalarGridSpec(
            num_scalar_prefetch=1,
            grid=(steps,),
            in_specs=[pl.BlockSpec((1, BLK * OPM, SEQS), lambda k, at: (k, 0, 0))] + in_specs,
            out_specs=[pl.BlockSpec((BLK, COLS, 128), lambda k, at: (where(k, at[0], at[1]), 0, 0))] + extra_specs,
            scratch_shapes=scratch + [pltpu.VMEM((BLK, 512, 384), BF16)],
        ),
        input_output_aliases=aliases,
        cost_estimate=pl.CostEstimate(flops=flops, bytes_accessed=8 * 1024 * 1024, transcendentals=0),
        compiler_params=VMEM,
        name="pair_grid",
    )(*operands)


def pair_first(place, left, own, other, weights):
    right = (OPM // 2, SEQS, 384)
    return pair_call(
        first_pair_kernel, lambda k, x_lo, y: x_lo * 4 + y, 1, (place, left, own, other) + weights,
        [whole(HALF, SEQS)] * 2 + [vmem_spec()] * 2,
        [jax.ShapeDtypeStruct(right, BF16)], [vmem_spec()], [pltpu.VMEM((2 * HALF, SEQS), F32)], {},
    )


def pair_next(place, left, right, weights, before, where):
    return pair_call(
        next_pair_kernel, where, left.shape[0], (place, left, right) + weights + (before,),
        [vmem_spec()] * 3 + [pl.BlockSpec(memory_space=pl.ANY)],
        [], [], [], {5: 0},
    )[0]


def crossed():
    pairs = []
    for d in range(SEQS):
        y, x_lo, core, z, x_hi = d % 4, d // 4 % 2, d // 8 % 2, d // 16 % 4, d // 64
        pairs.append((d, ((x_lo * 4 + y) * 2 + core) * 8 + x_hi * 4 + z))
    return pairs


def flipped(size, bit):
    return [(i, i ^ bit) for i in range(size)]


def body(alignment, w_query, w_key, w_value, w_gate, w_attend, w_left, w_right, w_pair):
    one = jax.ShapeDtypeStruct((SEQS, ROWS, LANES), BF16)
    packed = pl.pallas_call(
        pack_kernel, out_shape=one, in_specs=[vmem_spec()], out_specs=vmem_spec(),
        compiler_params=VMEM, name="pack",
    )(alignment[0])
    blocks = lax.all_to_all(packed, AXES, split_axis=0, concat_axis=0, tiled=True)
    w_sides = jnp.concatenate([w_left, w_right], axis=1).T
    w_pairs = w_pair.reshape(OPM, OPM // 2, 2, 128).transpose(2, 3, 1, 0).reshape(2, 128, 512)
    place = jnp.stack([lax.axis_index(a) for a in ("x_lo", "y", "core")]).astype(jnp.int32)
    blocks, w_even, w_odd, place = lax.optimization_barrier((blocks, w_pairs[0], w_pairs[1], place))
    weights = (w_even, w_odd)
    updated, left, right = attention(blocks, jnp.stack([w_query, w_key, w_value, w_gate, w_attend]), w_sides)

    own = lax.all_to_all(right, ("x_hi", "z"), split_axis=0, concat_axis=0, tiled=True)
    near = lax.ppermute(left, AXES, crossed())[None]
    near, own = lax.optimization_barrier((near, own))
    own = own.reshape(HALF, SEQS)
    other = lax.ppermute(own, "core", flipped(2, 1))
    returned = lax.all_to_all(updated, AXES, split_axis=0, concat_axis=0, tiled=True)
    second = lax.ppermute(near, "y", flipped(4, 2))
    grid, rights = pair_first(place, near, own, other, weights)

    second, grid = lax.optimization_barrier((second, grid))
    two = jnp.concatenate([near, second])
    third = lax.ppermute(two, "y", flipped(4, 1))
    fourth = lax.ppermute(two, "x_lo", flipped(2, 1))
    grid = pair_next(place, second, rights, weights, grid, lambda k, x_lo, y: x_lo * 4 + (y ^ 2))
    last = lax.ppermute(third, "x_lo", flipped(2, 1))
    grid = pair_next(place, third, rights, weights, grid, lambda k, x_lo, y: x_lo * 4 + (y ^ 1 ^ (k << 1)))
    grid = pair_next(place, fourth, rights, weights, grid, lambda k, x_lo, y: (1 - x_lo) * 4 + (y ^ (k << 1)))
    pair_update = pair_next(
        place, last, rights, weights, grid, lambda k, x_lo, y: (1 - x_lo) * 4 + (y ^ 1 ^ (k << 1))
    )
    returned, pair_update = lax.optimization_barrier((returned, pair_update))
    alignment_out = pl.pallas_call(
        unpack_kernel, out_shape=jax.ShapeDtypeStruct(alignment.shape[1:], BF16),
        in_specs=[vmem_spec()], out_specs=vmem_spec(), compiler_params=VMEM, name="unpack",
    )(returned)
    return (alignment_out[None], pair_update)


def solution(mesh):
    fine = Mesh(mesh.devices.reshape(SIZES), AXES)
    placed = (P(AXES, None, None),) + (P(),) * 8
    return jax.shard_map(
        body,
        mesh=fine,
        in_specs=placed,
        out_specs=(P(AXES, None, None), P(AXES[:3], AXES[3:], None)),
        check_vma=False,
    )
```

```python
import functools

import jax
import jax.numpy as jnp
from jax import lax
from jax.experimental import pallas as pl
from jax.experimental.pallas import tpu as pltpu
from jax.sharding import Mesh, PartitionSpec as P

HEADS = 8
HEAD_DIM = 32
OPM = 32
SEQS = 128
WIDTH = 256
LANES = 128
AXES = ("x_hi", "z", "core", "x_lo", "y")
SIZES = (2, 4, 2, 2, 4)
BLK = 12
ROWS = 2 * BLK
PEERS = 8
VMEM = pltpu.CompilerParams(vmem_limit_bytes=24 * 1024 * 1024)
F32 = jnp.float32
BF16 = jnp.bfloat16
NT = (((1,), (1,)), ((), ()))


def block_of(device):
    y, rest = device % 4, device // 4
    x_lo, rest = rest % 2, rest // 2
    core, rest = rest % 2, rest // 2
    z, x_hi = rest % 4, rest // 4
    return (x_lo * 4 + y) * 16 + core * 8 + x_hi * 4 + z


BLOCK_OF = [block_of(d) for d in range(SEQS)]
DEVICE_OF = [BLOCK_OF.index(b) for b in range(SEQS)]


def vmem_spec():
    return pl.BlockSpec(memory_space=pltpu.VMEM)


def normalise(values):
    average = jnp.mean(values, axis=-1, keepdims=True)
    centered = values - average
    variance = jnp.mean(centered * centered, axis=-1, keepdims=True)
    return (centered * lax.rsqrt(variance + 1e-05)).astype(BF16)


def pack_kernel(x_ref, out_ref):
    for group in range(SEQS // 4):
        rows = x_ref[group * 48 : group * 48 + 48, :].astype(F32)
        for part in range(4):
            piece = rows[part * BLK : part * BLK + BLK]
            both = jnp.concatenate([piece[:, :LANES], piece[:, LANES:]], axis=0)
            out_ref[DEVICE_OF[group * 4 + part]] = both.astype(BF16)


def unpack_kernel(x_ref, out_ref):
    for group in range(SEQS // 4):
        pieces = [x_ref[DEVICE_OF[group * 4 + part]].astype(F32) for part in range(4)]
        left = jnp.concatenate([piece[:BLK] for piece in pieces], axis=0)
        right = jnp.concatenate([piece[BLK:] for piece in pieces], axis=0)
        out_ref[group * 48 : group * 48 + 48, :] = jnp.concatenate([left, right], axis=1).astype(BF16)


def attention_kernel(
    x_ref, w_ref, wlr_ref, u_ref, lt_ref, rt_ref,
    flat, normed, query, key, value, gate, attended, update,
):
    flat[...] = x_ref[...].astype(F32).reshape(SEQS * ROWS, LANES)

    def residue(r):
        return jnp.concatenate(
            [flat[pl.ds(r, SEQS, stride=ROWS), :], flat[pl.ds(BLK + r, SEQS, stride=ROWS), :]], axis=1
        )

    def span(r):
        return pl.ds(r * SEQS, SEQS)

    for r in range(BLK):
        normed[span(r), :] = normalise(residue(r))
    rows = normed[...]
    query[...] = jnp.dot(rows, w_ref[0], preferred_element_type=F32).astype(BF16)
    key[...] = jnp.dot(rows, w_ref[1], preferred_element_type=F32).astype(BF16)
    value[...] = jnp.dot(rows, w_ref[2], preferred_element_type=F32).astype(BF16)
    gate[...] = jax.nn.sigmoid(jnp.dot(rows, w_ref[3], preferred_element_type=F32))

    lane = lax.broadcasted_iota(jnp.int32, (SEQS, WIDTH), 1) // HEAD_DIM
    own = [(lane == h) for h in range(HEADS)]
    zero = jnp.zeros((SEQS, WIDTH), BF16)
    ones = jnp.concatenate([jnp.where(m, 1.0, 0.0).astype(BF16) for m in own], axis=0)

    for r in range(BLK):
        at = span(r)
        q, k, v = query[at, :], key[at, :], value[at, :]
        k_heads = jnp.concatenate([jnp.where(m, k, zero) for m in own], axis=0)
        v_heads = jnp.concatenate([jnp.where(m, v, zero) for m in own], axis=0)
        scores = lax.dot_general(q, k_heads, NT, preferred_element_type=F32) * HEAD_DIM ** (-0.5)
        weighted = jnp.exp(scores).astype(BF16)
        numerator = jnp.dot(weighted, v_heads, preferred_element_type=F32)
        denominator = jnp.dot(weighted, ones, preferred_element_type=F32)
        attended[at, :] = (gate[at, :] * numerator / denominator).astype(BF16)

    update[...] = jnp.dot(attended[...], w_ref[4], preferred_element_type=F32)
    for r in range(BLK):
        updated = (residue(r) + update[span(r), :]).astype(BF16).astype(F32)
        flat[pl.ds(r, SEQS, stride=ROWS), :] = updated[:, :LANES]
        flat[pl.ds(BLK + r, SEQS, stride=ROWS), :] = updated[:, LANES:]
        normed[span(r), :] = normalise(updated)
    sides = lax.dot_general(wlr_ref[...], normed[...], NT, preferred_element_type=F32).astype(BF16)
    for r in range(BLK):
        lt_ref[r * OPM : (r + 1) * OPM, :] = sides[:OPM, r * SEQS : (r + 1) * SEQS]
        rt_ref[r * OPM : (r + 1) * OPM, :] = sides[OPM:, r * SEQS : (r + 1) * SEQS]
    u_ref[...] = flat[...].reshape(SEQS, ROWS, LANES).astype(BF16)


def attention(x, weights, wlr):
    tall = SEQS * BLK
    return pl.pallas_call(
        attention_kernel,
        out_shape=(
            jax.ShapeDtypeStruct((SEQS, ROWS, LANES), BF16),
            jax.ShapeDtypeStruct((BLK * OPM, SEQS), BF16),
            jax.ShapeDtypeStruct((BLK * OPM, SEQS), BF16),
        ),
        in_specs=[vmem_spec()] * 3,
        out_specs=(vmem_spec(),) * 3,
        scratch_shapes=[
            pltpu.VMEM((SEQS * ROWS, LANES), F32),
            pltpu.VMEM((tall, WIDTH), BF16),
            pltpu.VMEM((tall, WIDTH), BF16),
            pltpu.VMEM((tall, WIDTH), BF16),
            pltpu.VMEM((tall, WIDTH), BF16),
            pltpu.VMEM((tall, WIDTH), F32),
            pltpu.VMEM((tall, WIDTH), BF16),
            pltpu.VMEM((tall, WIDTH), F32),
        ],
        compiler_params=VMEM,
        name="attention",
    )(x, weights, wlr)


COLS = 192
HALF = PEERS * BLK * OPM


def pair_rows(left, right, we_ref, wo_ref, out_ref, outer):
    for p in range(OPM // 2):
        product = jnp.dot(left, right[p], preferred_element_type=F32).astype(BF16)
        for i in range(BLK):
            outer[i, p * OPM : (p + 1) * OPM, :] = product[i * OPM : (i + 1) * OPM]
    even_w, odd_w = we_ref[...], wo_ref[...]
    for i in range(BLK):
        even = jnp.dot(even_w, outer[i, :, :256], preferred_element_type=F32)
        odd = jnp.dot(odd_w, outer[i, :, 128:], preferred_element_type=F32)
        total = (even.T[:COLS] + odd.T[64:]) * (1.0 / SEQS)
        out_ref[i] = total.astype(BF16)


def first_pair_kernel(at_ref, l_ref, *refs):
    pieces, (we_ref, wo_ref, out_ref, right, flat, outer) = refs[:8], refs[8:]
    step = BLK * OPM

    @pl.when(pl.program_id(0) == 0)
    def _():
        for n, piece in enumerate(pieces):
            core = at_ref[2] ^ (n // 4)
            z = (at_ref[4] + (0, 3, 1, 2)[n % 4]) & 3
            for b in range(2):
                block = core * 8 + (at_ref[3] ^ b) * 4 + z
                flat[pl.ds(pl.multiple_of(block * step, step), step), :] = piece[b].astype(F32)
        for p in range(OPM // 2):
            even = flat[pl.ds(2 * p, COLS, stride=OPM), :]
            odd = flat[pl.ds(2 * p + 1, COLS, stride=OPM), :]
            right[p] = jnp.concatenate([even, odd], axis=0).T.astype(BF16)

    pair_rows(l_ref[0], right, we_ref, wo_ref, out_ref, outer)


def next_pair_kernel(at_ref, l_ref, right, we_ref, wo_ref, before_ref, out_ref, outer):
    pair_rows(l_ref[0], right, we_ref, wo_ref, out_ref, outer)


def whole(*shape):
    return pl.BlockSpec(shape, lambda k, at: (0,) * len(shape))


def pair_call(kernel, where, steps, operands, in_specs, extra_shapes, extra_specs, scratch, aliases):
    return pl.pallas_call(
        kernel,
        out_shape=[jax.ShapeDtypeStruct((PEERS * BLK, COLS, 128), BF16)] + extra_shapes,
        grid_spec=pltpu.PrefetchScalarGridSpec(
            num_scalar_prefetch=1,
            grid=(steps,),
            in_specs=[pl.BlockSpec((1, BLK * OPM, SEQS), lambda k, at: (k, 0, 0))] + in_specs,
            out_specs=[pl.BlockSpec((BLK, COLS, 128), lambda k, at: (where(k, at[0], at[1]), 0, 0))] + extra_specs,
            scratch_shapes=scratch + [pltpu.VMEM((BLK, 512, 384), BF16)],
        ),
        input_output_aliases=aliases,
        cost_estimate=pl.CostEstimate(flops=1000, bytes_accessed=1000, transcendentals=0),
        compiler_params=VMEM,
        name="pair_grid",
    )(*operands)


def pair_first(place, left, pieces, weights):
    right = (OPM // 2, SEQS, 384)
    return pair_call(
        first_pair_kernel, lambda k, x_lo, y: x_lo * 4 + (y ^ (k << 1)), 2, (place, left) + pieces + weights,
        [whole(*piece.shape) for piece in pieces] + [vmem_spec()] * 2,
        [jax.ShapeDtypeStruct(right, BF16)], [vmem_spec()], [pltpu.VMEM((2 * HALF, SEQS), F32)], {},
    )


def pair_next(place, left, right, weights, before, where):
    return pair_call(
        next_pair_kernel, where, left.shape[0], (place, left, right) + weights + (before,),
        [vmem_spec()] * 3 + [pl.BlockSpec(memory_space=pl.ANY)],
        [], [], [], {5: 0},
    )[0]


def crossed():
    pairs = []
    for d in range(SEQS):
        y, x_lo, core, z, x_hi = d % 4, d // 4 % 2, d // 8 % 2, d // 16 % 4, d // 64
        pairs.append((d, ((x_lo * 4 + y) * 2 + core) * 8 + x_hi * 4 + z))
    return pairs


def shifted(step):
    return [(i, (i + step) % 4) for i in range(4)]


def flipped(size, bit):
    return [(i, i ^ bit) for i in range(size)]


def body(alignment, w_query, w_key, w_value, w_gate, w_attend, w_left, w_right, w_pair):
    one = jax.ShapeDtypeStruct((SEQS, ROWS, LANES), BF16)
    packed = pl.pallas_call(
        pack_kernel, out_shape=one, in_specs=[vmem_spec()], out_specs=vmem_spec(),
        compiler_params=VMEM, name="pack",
    )(alignment[0])
    blocks = lax.all_to_all(packed, AXES, split_axis=0, concat_axis=0, tiled=True)
    w_sides = jnp.concatenate([w_left, w_right], axis=1).T
    w_pairs = w_pair.reshape(OPM, OPM // 2, 2, 128).transpose(2, 3, 1, 0).reshape(2, 128, 512)
    place = jnp.stack([lax.axis_index(a) for a in ("x_lo", "y", "core", "x_hi", "z")]).astype(jnp.int32)
    blocks, w_even, w_odd, place = lax.optimization_barrier((blocks, w_pairs[0], w_pairs[1], place))
    weights = (w_even, w_odd)
    updated, left, right = attention(blocks, jnp.stack([w_query, w_key, w_value, w_gate, w_attend]), w_sides)

    near = lax.ppermute(left, AXES, crossed())[None]
    mine = right[None]
    mine = jnp.concatenate([mine, lax.ppermute(mine, "x_hi", flipped(2, 1))])
    second = lax.ppermute(near, "y", flipped(4, 2))
    pieces = (mine, lax.ppermute(mine, "z", shifted(1)), lax.ppermute(mine, "z", shifted(3)), lax.ppermute(mine, "z", flipped(4, 2)))
    pieces, second, updated = lax.optimization_barrier((pieces, second, updated))
    pieces += tuple(lax.ppermute(piece, "core", flipped(2, 1)) for piece in pieces)
    returned = lax.all_to_all(updated, AXES, split_axis=0, concat_axis=0, tiled=True)

    two = jnp.concatenate([near, second])
    third = lax.ppermute(two, "y", flipped(4, 1))
    fourth = lax.ppermute(two, "x_lo", flipped(2, 1))
    grid, rights = pair_first(place, two, pieces, weights)
    third, grid = lax.optimization_barrier((third, grid))
    last = lax.ppermute(third, "x_lo", flipped(2, 1))
    grid = pair_next(place, third, rights, weights, grid, lambda k, x_lo, y: x_lo * 4 + (y ^ 1 ^ (k << 1)))
    grid = pair_next(place, fourth, rights, weights, grid, lambda k, x_lo, y: (1 - x_lo) * 4 + (y ^ (k << 1)))
    pair_update = pair_next(
        place, last, rights, weights, grid, lambda k, x_lo, y: (1 - x_lo) * 4 + (y ^ 1 ^ (k << 1))
    )
    returned, pair_update = lax.optimization_barrier((returned, pair_update))
    alignment_out = pl.pallas_call(
        unpack_kernel, out_shape=jax.ShapeDtypeStruct(alignment.shape[1:], BF16),
        in_specs=[vmem_spec()], out_specs=vmem_spec(), compiler_params=VMEM, name="unpack",
    )(returned)
    return (alignment_out[None], pair_update)


def solution(mesh):
    fine = Mesh(mesh.devices.reshape(SIZES), AXES)
    placed = (P(AXES, None, None),) + (P(),) * 8
    return jax.shard_map(
        body,
        mesh=fine,
        in_specs=placed,
        out_specs=(P(AXES, None, None), P(AXES[:3], AXES[3:], None)),
        check_vma=False,
    )
```

```python
import functools

import jax
import jax.numpy as jnp
from jax import lax
from jax.experimental import pallas as pl
from jax.experimental.pallas import tpu as pltpu
from jax.sharding import Mesh, PartitionSpec as P

HEADS = 8
HEAD_DIM = 32
OPM = 32
SEQS = 128
WIDTH = 256
LANES = 128
AXES = ("x_hi", "z", "core", "x_lo", "y")
SIZES = (2, 4, 2, 2, 4)
BLK = 12
ROWS = 2 * BLK
PEERS = 8
VMEM = pltpu.CompilerParams(vmem_limit_bytes=24 * 1024 * 1024)
F32 = jnp.float32
BF16 = jnp.bfloat16
NT = (((1,), (1,)), ((), ()))


def block_of(device):
    y, rest = device % 4, device // 4
    x_lo, rest = rest % 2, rest // 2
    core, rest = rest % 2, rest // 2
    z, x_hi = rest % 4, rest // 4
    return (x_lo * 4 + y) * 16 + core * 8 + x_hi * 4 + z


BLOCK_OF = [block_of(d) for d in range(SEQS)]
DEVICE_OF = [BLOCK_OF.index(b) for b in range(SEQS)]


def vmem_spec():
    return pl.BlockSpec(memory_space=pltpu.VMEM)


def normalise(values):
    average = jnp.mean(values, axis=-1, keepdims=True)
    centered = values - average
    variance = jnp.mean(centered * centered, axis=-1, keepdims=True)
    return (centered * lax.rsqrt(variance + 1e-05)).astype(BF16)


def pack_kernel(x_ref, out_ref):
    for group in range(SEQS // 4):
        rows = x_ref[group * 48 : group * 48 + 48, :].astype(F32)
        for part in range(4):
            piece = rows[part * BLK : part * BLK + BLK]
            both = jnp.concatenate([piece[:, :LANES], piece[:, LANES:]], axis=0)
            out_ref[DEVICE_OF[group * 4 + part]] = both.astype(BF16)


def unpack_kernel(x_ref, out_ref):
    for group in range(SEQS // 4):
        pieces = [x_ref[DEVICE_OF[group * 4 + part]].astype(F32) for part in range(4)]
        left = jnp.concatenate([piece[:BLK] for piece in pieces], axis=0)
        right = jnp.concatenate([piece[BLK:] for piece in pieces], axis=0)
        out_ref[group * 48 : group * 48 + 48, :] = jnp.concatenate([left, right], axis=1).astype(BF16)


def head_sums(weighted, own):
    sides = []
    for first in (0, HEADS // 2):
        side = jnp.zeros((SEQS, LANES), F32)
        for h in range(first, first + HEADS // 2):
            total = jnp.sum(weighted[:, h * SEQS : (h + 1) * SEQS], axis=-1, keepdims=True)
            side = jnp.where(own[h - first][:, :LANES], total, side)
        sides.append(side)
    return jnp.concatenate(sides, axis=1)


def attention_kernel(
    x_ref, w_ref, wlr_ref, u_ref, lt_ref, rt_ref,
    flat, normed, query, key, value, gate, attended, update,
):
    flat[...] = x_ref[...].astype(F32).reshape(SEQS * ROWS, LANES)

    def residue(r):
        return jnp.concatenate(
            [flat[pl.ds(r, SEQS, stride=ROWS), :], flat[pl.ds(BLK + r, SEQS, stride=ROWS), :]], axis=1
        )

    def span(r):
        return pl.ds(r * SEQS, SEQS)

    for r in range(BLK):
        normed[span(r), :] = normalise(residue(r))
    rows = normed[...]
    query[...] = jnp.dot(rows, w_ref[0], preferred_element_type=F32).astype(BF16)
    key[...] = jnp.dot(rows, w_ref[1], preferred_element_type=F32).astype(BF16)
    value[...] = jnp.dot(rows, w_ref[2], preferred_element_type=F32).astype(BF16)
    gate[...] = jax.nn.sigmoid(jnp.dot(rows, w_ref[3], preferred_element_type=F32))

    lane = lax.broadcasted_iota(jnp.int32, (SEQS, WIDTH), 1) // HEAD_DIM
    own = [(lane == h) for h in range(HEADS)]
    zero = jnp.zeros((SEQS, WIDTH), BF16)
    for r in range(BLK):
        at = span(r)
        q, k, v = query[at, :], key[at, :], value[at, :]
        k_heads = jnp.concatenate([jnp.where(m, k, zero) for m in own], axis=0)
        v_heads = jnp.concatenate([jnp.where(m, v, zero) for m in own], axis=0)
        scores = lax.dot_general(q, k_heads, NT, preferred_element_type=F32) * HEAD_DIM ** (-0.5)
        weighted = jnp.exp(scores).astype(BF16)
        numerator = jnp.dot(weighted, v_heads, preferred_element_type=F32)
        denominator = head_sums(weighted.astype(F32), own)
        attended[at, :] = (gate[at, :] * numerator / denominator).astype(BF16)

    update[...] = jnp.dot(attended[...], w_ref[4], preferred_element_type=F32)
    for r in range(BLK):
        updated = (residue(r) + update[span(r), :]).astype(BF16).astype(F32)
        flat[pl.ds(r, SEQS, stride=ROWS), :] = updated[:, :LANES]
        flat[pl.ds(BLK + r, SEQS, stride=ROWS), :] = updated[:, LANES:]
        normed[span(r), :] = normalise(updated)
    sides = lax.dot_general(wlr_ref[...], normed[...], NT, preferred_element_type=F32).astype(BF16)
    for r in range(BLK):
        lt_ref[r * OPM : (r + 1) * OPM, :] = sides[:OPM, r * SEQS : (r + 1) * SEQS]
        rt_ref[r * OPM : (r + 1) * OPM, :] = sides[OPM:, r * SEQS : (r + 1) * SEQS]
    u_ref[...] = flat[...].reshape(SEQS, ROWS, LANES).astype(BF16)


def attention(x, weights, wlr):
    tall = SEQS * BLK
    return pl.pallas_call(
        attention_kernel,
        out_shape=(
            jax.ShapeDtypeStruct((SEQS, ROWS, LANES), BF16),
            jax.ShapeDtypeStruct((BLK * OPM, SEQS), BF16),
            jax.ShapeDtypeStruct((BLK * OPM, SEQS), BF16),
        ),
        in_specs=[vmem_spec()] * 3,
        out_specs=(vmem_spec(),) * 3,
        scratch_shapes=[
            pltpu.VMEM((SEQS * ROWS, LANES), F32),
            pltpu.VMEM((tall, WIDTH), BF16),
            pltpu.VMEM((tall, WIDTH), BF16),
            pltpu.VMEM((tall, WIDTH), BF16),
            pltpu.VMEM((tall, WIDTH), BF16),
            pltpu.VMEM((tall, WIDTH), F32),
            pltpu.VMEM((tall, WIDTH), BF16),
            pltpu.VMEM((tall, WIDTH), F32),
        ],
        compiler_params=VMEM,
        name="attention",
    )(x, weights, wlr)


COLS = 192
PART = 4
HALF = PEERS * BLK * OPM


def pair_rows(at_ref, places, l_refs, right, we_ref, wo_ref, out_ref, outer, rows, sems):
    even_w, odd_w = we_ref[...], wo_ref[...]
    copies = []
    for turn, l_ref in enumerate(l_refs):
        left = l_ref[...].reshape(2 * BLK * OPM, SEQS)
        for p in range(OPM // 2):
            product = jnp.dot(left, right[p], preferred_element_type=F32).astype(BF16)
            for i in range(2 * BLK):
                outer[i, p * OPM : (p + 1) * OPM, :] = product[i * OPM : (i + 1) * OPM]
        for part in range(2 * BLK // PART):
            first = turn * 2 * BLK + part * PART
            for i in range(part * PART, part * PART + PART):
                even = jnp.dot(even_w, outer[i, :, :256], preferred_element_type=F32)
                odd = jnp.dot(odd_w, outer[i, :, 128:], preferred_element_type=F32)
                rows[turn * 2 * BLK + i] = ((even.T[:COLS] + odd.T[64:]) * (1.0 / SEQS)).astype(BF16)
            x_lo, y = places[first // BLK]
            target = ((at_ref[0] ^ x_lo) * 4 + (at_ref[1] ^ y)) * BLK + first % BLK
            copy = pltpu.make_async_copy(
                rows.at[pl.ds(first, PART)], out_ref.at[pl.ds(target, PART)], sems.at[first // PART]
            )
            copy.start()
            copies.append(copy)
    for copy in copies:
        copy.wait()


def first_pair_kernel(places, at_ref, l0_ref, l1_ref, *refs):
    pieces, (we_ref, wo_ref, out_ref, right, flat, outer, rows, sems) = refs[:8], refs[8:]
    step = BLK * OPM
    for n, piece in enumerate(pieces):
        for x in range(2):
            block = (at_ref[2] ^ (n // 4)) * 8 + (at_ref[3] ^ x) * 4 + (at_ref[4] ^ (n % 4))
            flat[pl.ds(pl.multiple_of(block * step, step), step), :] = piece[x].astype(F32)
    for p in range(OPM // 2):
        even = flat[pl.ds(2 * p, COLS, stride=OPM), :]
        odd = flat[pl.ds(2 * p + 1, COLS, stride=OPM), :]
        right[p] = jnp.concatenate([even, odd], axis=0).T.astype(BF16)
    pair_rows(at_ref, places, (l0_ref, l1_ref), right, we_ref, wo_ref, out_ref, outer, rows, sems)


def next_pair_kernel(places, at_ref, l0_ref, l1_ref, right, we_ref, wo_ref, before_ref, out_ref, outer, rows, sems):
    pair_rows(at_ref, places, (l0_ref, l1_ref), right, we_ref, wo_ref, out_ref, outer, rows, sems)


def pair_call(kernel, places, operands, in_specs, extra_shapes, scratch, aliases, flops):
    anywhere = pl.BlockSpec(memory_space=pl.ANY)
    return pl.pallas_call(
        functools.partial(kernel, places),
        out_shape=[jax.ShapeDtypeStruct((PEERS * BLK, COLS, 128), BF16)] + extra_shapes,
        in_specs=[pl.BlockSpec(memory_space=pltpu.SMEM)] + in_specs,
        out_specs=[anywhere] + [vmem_spec()] * len(extra_shapes),
        scratch_shapes=scratch
        + [
            pltpu.VMEM((2 * BLK, 512, 384), BF16),
            pltpu.VMEM((4 * BLK, COLS, 128), BF16),
            pltpu.SemaphoreType.DMA((4 * BLK // PART,)),
        ],
        input_output_aliases=aliases,
        cost_estimate=pl.CostEstimate(flops=flops, bytes_accessed=1000, transcendentals=0),
        compiler_params=VMEM,
        name="pair_grid",
    )(*operands)


def pair_first(place, lefts, pieces, weights, places):
    return pair_call(
        first_pair_kernel, places, (place,) + lefts + pieces + weights, [vmem_spec()] * 12,
        [jax.ShapeDtypeStruct((OPM // 2, SEQS, 384), BF16)], [pltpu.VMEM((2 * HALF, SEQS), F32)], {}, 40_000_000_000,
    )


def pair_next(place, lefts, right, weights, before, places):
    return pair_call(
        next_pair_kernel, places, (place,) + lefts + (right,) + weights + (before,),
        [vmem_spec()] * 5 + [pl.BlockSpec(memory_space=pl.ANY)], [], [], {6: 0}, 1000,
    )[0]


def crossed():
    pairs = []
    for d in range(SEQS):
        y, x_lo, core, z, x_hi = d % 4, d // 4 % 2, d // 8 % 2, d // 16 % 4, d // 64
        pairs.append((d, ((x_lo * 4 + y) * 2 + core) * 8 + x_hi * 4 + z))
    return pairs


def flipped(size, bit):
    return [(i, i ^ bit) for i in range(size)]


def body(alignment, w_query, w_key, w_value, w_gate, w_attend, w_left, w_right, w_pair):
    one = jax.ShapeDtypeStruct((SEQS, ROWS, LANES), BF16)
    packed = pl.pallas_call(
        pack_kernel, out_shape=one, in_specs=[vmem_spec()], out_specs=vmem_spec(),
        compiler_params=VMEM, name="pack",
    )(alignment[0])
    blocks = lax.all_to_all(packed, AXES, split_axis=0, concat_axis=0, tiled=True)
    w_sides = jnp.concatenate([w_left, w_right], axis=1).T
    w_pairs = w_pair.reshape(OPM, OPM // 2, 2, 128).transpose(2, 3, 1, 0).reshape(2, 128, 512)
    place = jnp.stack([lax.axis_index(a) for a in ("x_lo", "y", "core", "x_hi", "z")]).astype(jnp.int32)
    blocks, w_even, w_odd, place = lax.optimization_barrier((blocks, w_pairs[0], w_pairs[1], place))
    weights = (w_even, w_odd)
    updated, left, right = attention(blocks, jnp.stack([w_query, w_key, w_value, w_gate, w_attend]), w_sides)

    near = lax.ppermute(left, AXES, crossed())[None]
    two = jnp.concatenate([near, lax.ppermute(near, "y", flipped(4, 1))])
    more = lax.ppermute(two, "y", flipped(4, 3))
    mine = right[None]
    mine = jnp.concatenate([mine, lax.ppermute(mine, "x_hi", flipped(2, 1))])
    pieces = (mine, lax.ppermute(mine, "z", flipped(4, 1)), lax.ppermute(mine, "z", flipped(4, 2)), lax.ppermute(mine, "z", flipped(4, 3)))
    pieces, more, updated = lax.optimization_barrier((pieces, more, updated))
    others = tuple(lax.ppermute(piece, "core", flipped(2, 1)) for piece in pieces)
    updated, _ = lax.optimization_barrier((updated, others[0]))
    returned = lax.all_to_all(updated, AXES, split_axis=0, concat_axis=0, tiled=True)

    far = tuple(lax.ppermute(blocks, "x_lo", flipped(2, 1)) for blocks in (two, more))
    grid, rights = pair_first(place, (two, more), pieces + others, weights, ((0, 0), (0, 1), (0, 3), (0, 2)))
    pair_update = pair_next(place, far, rights, weights, grid, ((1, 0), (1, 1), (1, 3), (1, 2)))
    returned, pair_update = lax.optimization_barrier((returned, pair_update))
    alignment_out = pl.pallas_call(
        unpack_kernel, out_shape=jax.ShapeDtypeStruct(alignment.shape[1:], BF16),
        in_specs=[vmem_spec()], out_specs=vmem_spec(), compiler_params=VMEM, name="unpack",
    )(returned)
    return (alignment_out[None], pair_update)


def solution(mesh):
    fine = Mesh(mesh.devices.reshape(SIZES), AXES)
    placed = (P(AXES, None, None),) + (P(),) * 8
    return jax.shard_map(
        body,
        mesh=fine,
        in_specs=placed,
        out_specs=(P(AXES, None, None), P(AXES[:3], AXES[3:], None)),
        check_vma=False,
    )
```

```python
import functools

import jax
import jax.numpy as jnp
from jax import lax
from jax.experimental import pallas as pl
from jax.experimental.pallas import tpu as pltpu
from jax.sharding import Mesh, PartitionSpec as P

HEADS = 8
HEAD_DIM = 32
OPM = 32
SEQS = 128
WIDTH = 256
LANES = 128
AXES = ("x_hi", "z", "core", "x_lo", "y")
SIZES = (2, 4, 2, 2, 4)
BLK = 12
ROWS = 2 * BLK
PEERS = 8
VMEM = pltpu.CompilerParams(vmem_limit_bytes=24 * 1024 * 1024)
F32 = jnp.float32
BF16 = jnp.bfloat16
NT = (((1,), (1,)), ((), ()))


def block_of(device):
    y, rest = device % 4, device // 4
    x_lo, rest = rest % 2, rest // 2
    core, rest = rest % 2, rest // 2
    z, x_hi = rest % 4, rest // 4
    return (x_lo * 4 + y) * 16 + core * 8 + x_hi * 4 + z


BLOCK_OF = [block_of(d) for d in range(SEQS)]
DEVICE_OF = [BLOCK_OF.index(b) for b in range(SEQS)]


def vmem_spec():
    return pl.BlockSpec(memory_space=pltpu.VMEM)


def normalise(values):
    average = jnp.mean(values, axis=-1, keepdims=True)
    centered = values - average
    variance = jnp.mean(centered * centered, axis=-1, keepdims=True)
    return (centered * lax.rsqrt(variance + 1e-05)).astype(BF16)


def pack_kernel(x_ref, out_ref):
    for group in range(SEQS // 4):
        rows = x_ref[group * 48 : group * 48 + 48, :].astype(F32)
        for part in range(4):
            piece = rows[part * BLK : part * BLK + BLK]
            both = jnp.concatenate([piece[:, :LANES], piece[:, LANES:]], axis=0)
            out_ref[DEVICE_OF[group * 4 + part]] = both.astype(BF16)


def unpack_kernel(x_ref, out_ref):
    for group in range(SEQS // 4):
        pieces = [x_ref[DEVICE_OF[group * 4 + part]].astype(F32) for part in range(4)]
        left = jnp.concatenate([piece[:BLK] for piece in pieces], axis=0)
        right = jnp.concatenate([piece[BLK:] for piece in pieces], axis=0)
        out_ref[group * 48 : group * 48 + 48, :] = jnp.concatenate([left, right], axis=1).astype(BF16)


def head_sums(weighted, own):
    sides = []
    for first in (0, HEADS // 2):
        side = jnp.zeros((SEQS, LANES), F32)
        for h in range(first, first + HEADS // 2):
            total = jnp.sum(weighted[:, h * SEQS : (h + 1) * SEQS], axis=-1, keepdims=True)
            side = jnp.where(own[h - first][:, :LANES], total, side)
        sides.append(side)
    return jnp.concatenate(sides, axis=1)


def attention_kernel(
    x_ref, w_ref, wlr_ref, u_ref, lt_ref, rt_ref,
    flat, normed, query, key, value, gate, attended, update,
):
    flat[...] = x_ref[...].astype(F32).reshape(SEQS * ROWS, LANES)

    def residue(r):
        return jnp.concatenate(
            [flat[pl.ds(r, SEQS, stride=ROWS), :], flat[pl.ds(BLK + r, SEQS, stride=ROWS), :]], axis=1
        )

    def span(r):
        return pl.ds(r * SEQS, SEQS)

    for r in range(BLK):
        normed[span(r), :] = normalise(residue(r))
    rows = normed[...]
    query[...] = jnp.dot(rows, w_ref[0], preferred_element_type=F32).astype(BF16)
    key[...] = jnp.dot(rows, w_ref[1], preferred_element_type=F32).astype(BF16)
    value[...] = jnp.dot(rows, w_ref[2], preferred_element_type=F32).astype(BF16)
    gate[...] = jax.nn.sigmoid(jnp.dot(rows, w_ref[3], preferred_element_type=F32))

    lane = lax.broadcasted_iota(jnp.int32, (SEQS, WIDTH), 1) // HEAD_DIM
    own = [(lane == h) for h in range(HEADS)]
    zero = jnp.zeros((SEQS, WIDTH), BF16)
    for r in range(BLK):
        at = span(r)
        q, k, v = query[at, :], key[at, :], value[at, :]
        k_heads = jnp.concatenate([jnp.where(m, k, zero) for m in own], axis=0)
        v_heads = jnp.concatenate([jnp.where(m, v, zero) for m in own], axis=0)
        scores = lax.dot_general(q, k_heads, NT, preferred_element_type=F32) * HEAD_DIM ** (-0.5)
        weighted = jnp.exp(scores).astype(BF16)
        numerator = jnp.dot(weighted, v_heads, preferred_element_type=F32)
        denominator = head_sums(weighted.astype(F32), own)
        attended[at, :] = (gate[at, :] * numerator / denominator).astype(BF16)

    update[...] = jnp.dot(attended[...], w_ref[4], preferred_element_type=F32)
    for r in range(BLK):
        updated = (residue(r) + update[span(r), :]).astype(BF16).astype(F32)
        flat[pl.ds(r, SEQS, stride=ROWS), :] = updated[:, :LANES]
        flat[pl.ds(BLK + r, SEQS, stride=ROWS), :] = updated[:, LANES:]
        normed[span(r), :] = normalise(updated)
    sides = lax.dot_general(wlr_ref[...], normed[...], NT, preferred_element_type=F32).astype(BF16)
    for r in range(BLK):
        lt_ref[r * OPM : (r + 1) * OPM, :] = sides[:OPM, r * SEQS : (r + 1) * SEQS]
        rt_ref[r * OPM : (r + 1) * OPM, :] = sides[OPM:, r * SEQS : (r + 1) * SEQS]
    u_ref[...] = flat[...].reshape(SEQS, ROWS, LANES).astype(BF16)


def attention(x, weights, wlr):
    tall = SEQS * BLK
    return pl.pallas_call(
        attention_kernel,
        out_shape=(
            jax.ShapeDtypeStruct((SEQS, ROWS, LANES), BF16),
            jax.ShapeDtypeStruct((BLK * OPM, SEQS), BF16),
            jax.ShapeDtypeStruct((BLK * OPM, SEQS), BF16),
        ),
        in_specs=[vmem_spec()] * 3,
        out_specs=(vmem_spec(),) * 3,
        scratch_shapes=[
            pltpu.VMEM((SEQS * ROWS, LANES), F32),
            pltpu.VMEM((tall, WIDTH), BF16),
            pltpu.VMEM((tall, WIDTH), BF16),
            pltpu.VMEM((tall, WIDTH), BF16),
            pltpu.VMEM((tall, WIDTH), BF16),
            pltpu.VMEM((tall, WIDTH), F32),
            pltpu.VMEM((tall, WIDTH), BF16),
            pltpu.VMEM((tall, WIDTH), F32),
        ],
        compiler_params=VMEM,
        name="attention",
    )(x, weights, wlr)


COLS = 192
PART = 4
HALF = PEERS * BLK * OPM


def pair_rows(at_ref, places, l_refs, right, we_ref, wo_ref, out_ref, outer, rows, sems):
    even_w, odd_w = we_ref[...], wo_ref[...]
    copies = []
    for turn, l_ref in enumerate(l_refs):
        left = l_ref[...].reshape(2 * BLK * OPM, SEQS)
        for p in range(OPM // 2):
            product = jnp.dot(left, right[p], preferred_element_type=F32).astype(BF16)
            for i in range(2 * BLK):
                outer[i, p * OPM : (p + 1) * OPM, :] = product[i * OPM : (i + 1) * OPM]
        for part in range(2 * BLK // PART):
            first = turn * 2 * BLK + part * PART
            for i in range(part * PART, part * PART + PART):
                even = jnp.dot(even_w, outer[i, :, :256], preferred_element_type=F32)
                odd = jnp.dot(odd_w, outer[i, :, 128:], preferred_element_type=F32)
                rows[turn * 2 * BLK + i] = ((even.T[:COLS] + odd.T[64:]) * (1.0 / SEQS)).astype(BF16)
            x_lo, y = places[first // BLK]
            target = ((at_ref[0] ^ x_lo) * 4 + (at_ref[1] ^ y)) * BLK + first % BLK
            copy = pltpu.make_async_copy(
                rows.at[pl.ds(first, PART)], out_ref.at[pl.ds(target, PART)], sems.at[first // PART]
            )
            copy.start()
            copies.append(copy)
    for copy in copies:
        copy.wait()


def first_pair_kernel(places, at_ref, l_ref, *refs):
    pieces, (we_ref, wo_ref, out_ref, right, flat, outer, rows, sems) = refs[:8], refs[8:]
    step = BLK * OPM
    for n, piece in enumerate(pieces):
        for x in range(2):
            block = (at_ref[2] ^ (n // 4)) * 8 + (at_ref[3] ^ x) * 4 + (at_ref[4] ^ (n % 4))
            flat[pl.ds(pl.multiple_of(block * step, step), step), :] = piece[x].astype(F32)
    for p in range(OPM // 2):
        even = flat[pl.ds(2 * p, COLS, stride=OPM), :]
        odd = flat[pl.ds(2 * p + 1, COLS, stride=OPM), :]
        right[p] = jnp.concatenate([even, odd], axis=0).T.astype(BF16)
    pair_rows(at_ref, places, (l_ref,), right, we_ref, wo_ref, out_ref, outer, rows, sems)


def next_pair_kernel(places, at_ref, *refs):
    l_refs, (right, we_ref, wo_ref, before_ref, out_ref, outer, rows, sems) = refs[:-8], refs[-8:]
    pair_rows(at_ref, places, l_refs, right, we_ref, wo_ref, out_ref, outer, rows, sems)


def pair_call(kernel, places, operands, in_specs, extra_shapes, scratch, aliases, flops):
    anywhere = pl.BlockSpec(memory_space=pl.ANY)
    return pl.pallas_call(
        functools.partial(kernel, places),
        out_shape=[jax.ShapeDtypeStruct((PEERS * BLK, COLS, 128), BF16)] + extra_shapes,
        in_specs=[pl.BlockSpec(memory_space=pltpu.SMEM)] + in_specs,
        out_specs=[anywhere] + [vmem_spec()] * len(extra_shapes),
        scratch_shapes=scratch
        + [
            pltpu.VMEM((2 * BLK, 512, 384), BF16),
            pltpu.VMEM((4 * BLK, COLS, 128), BF16),
            pltpu.SemaphoreType.DMA((4 * BLK // PART,)),
        ],
        input_output_aliases=aliases,
        cost_estimate=pl.CostEstimate(flops=flops, bytes_accessed=1000, transcendentals=0),
        compiler_params=VMEM,
        name="pair_grid",
    )(*operands)


def pair_first(place, lefts, pieces, weights, places):
    return pair_call(
        first_pair_kernel, places, (place, lefts) + pieces + weights, [vmem_spec()] * 11,
        [jax.ShapeDtypeStruct((OPM // 2, SEQS, 384), BF16)], [pltpu.VMEM((2 * HALF, SEQS), F32)], {}, 40_000_000_000,
    )


def pair_next(place, lefts, right, weights, before, places):
    return pair_call(
        next_pair_kernel, places, (place,) + lefts + (right,) + weights + (before,),
        [vmem_spec()] * (3 + len(lefts)) + [pl.BlockSpec(memory_space=pl.ANY)], [], [], {4 + len(lefts): 0}, 1000,
    )[0]


def crossed():
    pairs = []
    for d in range(SEQS):
        y, x_lo, core, z, x_hi = d % 4, d // 4 % 2, d // 8 % 2, d // 16 % 4, d // 64
        pairs.append((d, ((x_lo * 4 + y) * 2 + core) * 8 + x_hi * 4 + z))
    return pairs


def flipped(size, bit):
    return [(i, i ^ bit) for i in range(size)]


def body(alignment, w_query, w_key, w_value, w_gate, w_attend, w_left, w_right, w_pair):
    one = jax.ShapeDtypeStruct((SEQS, ROWS, LANES), BF16)
    packed = pl.pallas_call(
        pack_kernel, out_shape=one, in_specs=[vmem_spec()], out_specs=vmem_spec(),
        compiler_params=VMEM, name="pack",
    )(alignment[0])
    blocks = lax.all_to_all(packed, AXES, split_axis=0, concat_axis=0, tiled=True)
    w_sides = jnp.concatenate([w_left, w_right], axis=1).T
    w_pairs = w_pair.reshape(OPM, OPM // 2, 2, 128).transpose(2, 3, 1, 0).reshape(2, 128, 512)
    place = jnp.stack([lax.axis_index(a) for a in ("x_lo", "y", "core", "x_hi", "z")]).astype(jnp.int32)
    blocks, w_even, w_odd, place = lax.optimization_barrier((blocks, w_pairs[0], w_pairs[1], place))
    weights = (w_even, w_odd)
    updated, left, right = attention(blocks, jnp.stack([w_query, w_key, w_value, w_gate, w_attend]), w_sides)

    near = lax.ppermute(left, AXES, crossed())[None]
    second = lax.ppermute(near, "y", flipped(4, 1))
    mine = right[None]
    mine = jnp.concatenate([mine, lax.ppermute(mine, "x_hi", flipped(2, 1))])
    pieces = (mine, lax.ppermute(mine, "z", flipped(4, 1)), lax.ppermute(mine, "z", flipped(4, 2)), lax.ppermute(mine, "z", flipped(4, 3)))
    pieces, second, updated = lax.optimization_barrier((pieces, second, updated))
    others = tuple(lax.ppermute(piece, "core", flipped(2, 1)) for piece in pieces)
    updated, _ = lax.optimization_barrier((updated, others[0]))
    returned = lax.all_to_all(updated, AXES, split_axis=0, concat_axis=0, tiled=True)

    two = jnp.concatenate([near, second])
    more = lax.ppermute(two, "y", flipped(4, 3))
    far = lax.ppermute(two, "x_lo", flipped(2, 1))
    grid, rights = pair_first(place, two, pieces + others, weights, ((0, 0), (0, 1)))
    more, grid = lax.optimization_barrier((more, grid))
    last = lax.ppermute(more, "x_lo", flipped(2, 1))
    grid = pair_next(place, (more, far), rights, weights, grid, ((0, 3), (0, 2), (1, 0), (1, 1)))
    pair_update = pair_next(place, (last,), rights, weights, grid, ((1, 3), (1, 2)))
    returned, pair_update = lax.optimization_barrier((returned, pair_update))
    alignment_out = pl.pallas_call(
        unpack_kernel, out_shape=jax.ShapeDtypeStruct(alignment.shape[1:], BF16),
        in_specs=[vmem_spec()], out_specs=vmem_spec(), compiler_params=VMEM, name="unpack",
    )(returned)
    return (alignment_out[None], pair_update)


def solution(mesh):
    fine = Mesh(mesh.devices.reshape(SIZES), AXES)
    placed = (P(AXES, None, None),) + (P(),) * 8
    return jax.shard_map(
        body,
        mesh=fine,
        in_specs=placed,
        out_specs=(P(AXES, None, None), P(AXES[:3], AXES[3:], None)),
        check_vma=False,
    )
```

```python
import functools

import jax
import jax.numpy as jnp
from jax import lax
from jax.experimental import pallas as pl
from jax.experimental.pallas import tpu as pltpu
from jax.sharding import Mesh, PartitionSpec as P

HEADS = 8
HEAD_DIM = 32
OPM = 32
SEQS = 128
WIDTH = 256
LANES = 128
AXES = ("x_hi", "z", "core", "x_lo", "y")
SIZES = (2, 4, 2, 2, 4)
BLK = 12
ROWS = 2 * BLK
PEERS = 8
VMEM = pltpu.CompilerParams(vmem_limit_bytes=24 * 1024 * 1024)
F32 = jnp.float32
BF16 = jnp.bfloat16
NT = (((1,), (1,)), ((), ()))


def block_of(device):
    y, rest = device % 4, device // 4
    x_lo, rest = rest % 2, rest // 2
    core, rest = rest % 2, rest // 2
    z, x_hi = rest % 4, rest // 4
    return (x_lo * 4 + y) * 16 + core * 8 + x_hi * 4 + z


BLOCK_OF = [block_of(d) for d in range(SEQS)]
DEVICE_OF = [BLOCK_OF.index(b) for b in range(SEQS)]


def vmem_spec():
    return pl.BlockSpec(memory_space=pltpu.VMEM)


def normalise(values):
    average = jnp.mean(values, axis=-1, keepdims=True)
    centered = values - average
    variance = jnp.mean(centered * centered, axis=-1, keepdims=True)
    return (centered * lax.rsqrt(variance + 1e-05)).astype(BF16)


def pack_kernel(x_ref, out_ref):
    for group in range(SEQS // 4):
        rows = x_ref[group * 48 : group * 48 + 48, :].astype(F32)
        for part in range(4):
            piece = rows[part * BLK : part * BLK + BLK]
            both = jnp.concatenate([piece[:, :LANES], piece[:, LANES:]], axis=0)
            out_ref[DEVICE_OF[group * 4 + part]] = both.astype(BF16)


def unpack_kernel(x_ref, out_ref):
    for group in range(SEQS // 4):
        pieces = [x_ref[DEVICE_OF[group * 4 + part]].astype(F32) for part in range(4)]
        left = jnp.concatenate([piece[:BLK] for piece in pieces], axis=0)
        right = jnp.concatenate([piece[BLK:] for piece in pieces], axis=0)
        out_ref[group * 48 : group * 48 + 48, :] = jnp.concatenate([left, right], axis=1).astype(BF16)


def head_sums(weighted, own):
    sides = []
    for first in (0, HEADS // 2):
        side = jnp.zeros((SEQS, LANES), F32)
        for h in range(first, first + HEADS // 2):
            total = jnp.sum(weighted[:, h * SEQS : (h + 1) * SEQS], axis=-1, keepdims=True)
            side = jnp.where(own[h - first][:, :LANES], total, side)
        sides.append(side)
    return jnp.concatenate(sides, axis=1)


def attention_kernel(
    x_ref, w_ref, wlr_ref, u_ref, lt_ref, rt_ref,
    flat, normed, query, key, value, gate, attended, update,
):
    flat[...] = x_ref[...].astype(F32).reshape(SEQS * ROWS, LANES)

    def residue(r):
        return jnp.concatenate(
            [flat[pl.ds(r, SEQS, stride=ROWS), :], flat[pl.ds(BLK + r, SEQS, stride=ROWS), :]], axis=1
        )

    def span(r):
        return pl.ds(r * SEQS, SEQS)

    for r in range(BLK):
        normed[span(r), :] = normalise(residue(r))
    rows = normed[...]
    query[...] = jnp.dot(rows, w_ref[0], preferred_element_type=F32).astype(BF16)
    key[...] = jnp.dot(rows, w_ref[1], preferred_element_type=F32).astype(BF16)
    value[...] = jnp.dot(rows, w_ref[2], preferred_element_type=F32).astype(BF16)
    gate[...] = jax.nn.sigmoid(jnp.dot(rows, w_ref[3], preferred_element_type=F32))

    lane = lax.broadcasted_iota(jnp.int32, (SEQS, WIDTH), 1) // HEAD_DIM
    own = [(lane == h) for h in range(HEADS)]
    zero = jnp.zeros((SEQS, WIDTH), BF16)
    for r in range(BLK):
        at = span(r)
        q, k, v = query[at, :], key[at, :], value[at, :]
        k_heads = jnp.concatenate([jnp.where(m, k, zero) for m in own], axis=0)
        v_heads = jnp.concatenate([jnp.where(m, v, zero) for m in own], axis=0)
        scores = lax.dot_general(q, k_heads, NT, preferred_element_type=F32) * HEAD_DIM ** (-0.5)
        weighted = jnp.exp(scores).astype(BF16)
        numerator = jnp.dot(weighted, v_heads, preferred_element_type=F32)
        denominator = head_sums(weighted.astype(F32), own)
        attended[at, :] = (gate[at, :] * numerator / denominator).astype(BF16)

    update[...] = jnp.dot(attended[...], w_ref[4], preferred_element_type=F32)
    for r in range(BLK):
        updated = (residue(r) + update[span(r), :]).astype(BF16).astype(F32)
        flat[pl.ds(r, SEQS, stride=ROWS), :] = updated[:, :LANES]
        flat[pl.ds(BLK + r, SEQS, stride=ROWS), :] = updated[:, LANES:]
        normed[span(r), :] = normalise(updated)
    sides = lax.dot_general(wlr_ref[...], normed[...], NT, preferred_element_type=F32).astype(BF16)
    for r in range(BLK):
        lt_ref[r * OPM : (r + 1) * OPM, :] = sides[:OPM, r * SEQS : (r + 1) * SEQS]
        rt_ref[r * OPM : (r + 1) * OPM, :] = sides[OPM:, r * SEQS : (r + 1) * SEQS]
    u_ref[...] = flat[...].reshape(SEQS, ROWS, LANES).astype(BF16)


def attention(x, weights, wlr):
    tall = SEQS * BLK
    return pl.pallas_call(
        attention_kernel,
        out_shape=(
            jax.ShapeDtypeStruct((SEQS, ROWS, LANES), BF16),
            jax.ShapeDtypeStruct((BLK * OPM, SEQS), BF16),
            jax.ShapeDtypeStruct((BLK * OPM, SEQS), BF16),
        ),
        in_specs=[vmem_spec()] * 3,
        out_specs=(vmem_spec(),) * 3,
        scratch_shapes=[
            pltpu.VMEM((SEQS * ROWS, LANES), F32),
            pltpu.VMEM((tall, WIDTH), BF16),
            pltpu.VMEM((tall, WIDTH), BF16),
            pltpu.VMEM((tall, WIDTH), BF16),
            pltpu.VMEM((tall, WIDTH), BF16),
            pltpu.VMEM((tall, WIDTH), F32),
            pltpu.VMEM((tall, WIDTH), BF16),
            pltpu.VMEM((tall, WIDTH), F32),
        ],
        compiler_params=VMEM,
        name="attention",
    )(x, weights, wlr)


COLS = 192
PART = 4
HALF = PEERS * BLK * OPM


def pair_rows(at_ref, places, l_refs, right, we_ref, wo_ref, out_ref, outer, rows, sems):
    even_w, odd_w = we_ref[...], wo_ref[...]
    copies = []
    for turn, l_ref in enumerate(l_refs):
        left = l_ref[...].reshape(2 * BLK * OPM, SEQS)
        for p in range(OPM // 2):
            product = jnp.dot(left, right[p], preferred_element_type=F32).astype(BF16)
            for i in range(2 * BLK):
                outer[i, p * OPM : (p + 1) * OPM, :] = product[i * OPM : (i + 1) * OPM]
        for part in range(2 * BLK // PART):
            first = turn * 2 * BLK + part * PART
            for i in range(part * PART, part * PART + PART):
                even = jnp.dot(even_w, outer[i, :, :256], preferred_element_type=F32)
                odd = jnp.dot(odd_w, outer[i, :, 128:], preferred_element_type=F32)
                rows[turn * 2 * BLK + i] = ((even.T[:COLS] + odd.T[64:]) * (1.0 / SEQS)).astype(BF16)
            x_lo, y = places[first // BLK]
            target = ((at_ref[0] ^ x_lo) * 4 + (at_ref[1] ^ y)) * BLK + first % BLK
            copy = pltpu.make_async_copy(
                rows.at[pl.ds(first, PART)], out_ref.at[pl.ds(target, PART)], sems.at[first // PART]
            )
            copy.start()
            copies.append(copy)
    for copy in copies:
        copy.wait()


def first_pair_kernel(places, at_ref, l_ref, *refs):
    pieces, (we_ref, wo_ref, out_ref, right, flat, outer, rows, sems) = refs[:8], refs[8:]
    step = BLK * OPM
    for n, piece in enumerate(pieces):
        for x in range(2):
            block = (at_ref[2] ^ (n // 4)) * 8 + (at_ref[3] ^ x) * 4 + (at_ref[4] ^ (n % 4))
            flat[pl.ds(pl.multiple_of(block * step, step), step), :] = piece[x].astype(F32)
    for p in range(OPM // 2):
        even = flat[pl.ds(2 * p, COLS, stride=OPM), :]
        odd = flat[pl.ds(2 * p + 1, COLS, stride=OPM), :]
        right[p] = jnp.concatenate([even, odd], axis=0).T.astype(BF16)
    pair_rows(at_ref, places, (l_ref,), right, we_ref, wo_ref, out_ref, outer, rows, sems)


def next_pair_kernel(places, at_ref, *refs):
    l_refs, (right, we_ref, wo_ref, before_ref, out_ref, outer, rows, sems) = refs[:-8], refs[-8:]
    pair_rows(at_ref, places, l_refs, right, we_ref, wo_ref, out_ref, outer, rows, sems)


def pair_call(kernel, places, operands, in_specs, extra_shapes, scratch, aliases, flops):
    anywhere = pl.BlockSpec(memory_space=pl.ANY)
    return pl.pallas_call(
        functools.partial(kernel, places),
        out_shape=[jax.ShapeDtypeStruct((PEERS * BLK, COLS, 128), BF16)] + extra_shapes,
        in_specs=[pl.BlockSpec(memory_space=pltpu.SMEM)] + in_specs,
        out_specs=[anywhere] + [vmem_spec()] * len(extra_shapes),
        scratch_shapes=scratch
        + [
            pltpu.VMEM((2 * BLK, 512, 384), BF16),
            pltpu.VMEM((4 * BLK, COLS, 128), BF16),
            pltpu.SemaphoreType.DMA((4 * BLK // PART,)),
        ],
        input_output_aliases=aliases,
        cost_estimate=pl.CostEstimate(flops=flops, bytes_accessed=1000, transcendentals=0),
        compiler_params=VMEM,
        name="pair_grid",
    )(*operands)


def pair_first(place, lefts, pieces, weights, places):
    return pair_call(
        first_pair_kernel, places, (place, lefts) + pieces + weights, [vmem_spec()] * 11,
        [jax.ShapeDtypeStruct((OPM // 2, SEQS, 384), BF16)], [pltpu.VMEM((2 * HALF, SEQS), F32)], {}, 40_000_000_000,
    )


def pair_next(place, lefts, right, weights, before, places):
    return pair_call(
        next_pair_kernel, places, (place,) + lefts + (right,) + weights + (before,),
        [vmem_spec()] * (3 + len(lefts)) + [pl.BlockSpec(memory_space=pl.ANY)], [], [], {4 + len(lefts): 0}, 1000,
    )[0]


def crossed():
    pairs = []
    for d in range(SEQS):
        y, x_lo, core, z, x_hi = d % 4, d // 4 % 2, d // 8 % 2, d // 16 % 4, d // 64
        pairs.append((d, ((x_lo * 4 + y) * 2 + core) * 8 + x_hi * 4 + z))
    return pairs


def flipped(size, bit):
    return [(i, i ^ bit) for i in range(size)]


def body(alignment, w_query, w_key, w_value, w_gate, w_attend, w_left, w_right, w_pair):
    one = jax.ShapeDtypeStruct((SEQS, ROWS, LANES), BF16)
    packed = pl.pallas_call(
        pack_kernel, out_shape=one, in_specs=[vmem_spec()], out_specs=vmem_spec(),
        compiler_params=VMEM, name="pack",
    )(alignment[0])
    blocks = lax.all_to_all(packed, AXES, split_axis=0, concat_axis=0, tiled=True)
    w_sides = jnp.concatenate([w_left, w_right], axis=1).T
    w_pairs = w_pair.reshape(OPM, OPM // 2, 2, 128).transpose(2, 3, 1, 0).reshape(2, 128, 512)
    place = jnp.stack([lax.axis_index(a) for a in ("x_lo", "y", "core", "x_hi", "z")]).astype(jnp.int32)
    blocks, w_even, w_odd, place = lax.optimization_barrier((blocks, w_pairs[0], w_pairs[1], place))
    weights = (w_even, w_odd)
    updated, left, right = attention(blocks, jnp.stack([w_query, w_key, w_value, w_gate, w_attend]), w_sides)

    near = lax.ppermute(left, AXES, crossed())[None]
    second = lax.ppermute(near, "y", flipped(4, 1))
    mine = right[None]
    mine = jnp.concatenate([mine, lax.ppermute(mine, "x_hi", flipped(2, 1))])
    z_1, z_3 = lax.ppermute(mine, "z", flipped(4, 1)), lax.ppermute(mine, "z", flipped(4, 3))
    z_2 = lax.ppermute(mine, "z", flipped(4, 2))
    (mine, z_1, z_3, z_2), second, updated = lax.optimization_barrier(((mine, z_1, z_3, z_2), second, updated))
    pieces = (mine, z_1, z_2, z_3)
    others = tuple(lax.ppermute(piece, "core", flipped(2, 1)) for piece in pieces)
    updated, _ = lax.optimization_barrier((updated, others[0]))
    returned = lax.all_to_all(updated, AXES, split_axis=0, concat_axis=0, tiled=True)

    two = jnp.concatenate([near, second])
    more = lax.ppermute(two, "y", flipped(4, 3))
    far = lax.ppermute(two, "x_lo", flipped(2, 1))
    grid, rights = pair_first(place, two, pieces + others, weights, ((0, 0), (0, 1)))
    more, grid = lax.optimization_barrier((more, grid))
    last = lax.ppermute(more, "x_lo", flipped(2, 1))
    grid = pair_next(place, (more, far), rights, weights, grid, ((0, 3), (0, 2), (1, 0), (1, 1)))
    pair_update = pair_next(place, (last,), rights, weights, grid, ((1, 3), (1, 2)))
    returned, pair_update = lax.optimization_barrier((returned, pair_update))
    alignment_out = pl.pallas_call(
        unpack_kernel, out_shape=jax.ShapeDtypeStruct(alignment.shape[1:], BF16),
        in_specs=[vmem_spec()], out_specs=vmem_spec(), compiler_params=VMEM, name="unpack",
    )(returned)
    return (alignment_out[None], pair_update)


def solution(mesh):
    fine = Mesh(mesh.devices.reshape(SIZES), AXES)
    placed = (P(AXES, None, None),) + (P(),) * 8
    return jax.shard_map(
        body,
        mesh=fine,
        in_specs=placed,
        out_specs=(P(AXES, None, None), P(AXES[:3], AXES[3:], None)),
        check_vma=False,
    )
```
